512 devices in a mesh: outer: 16 (over z_lo, x), inner: 32 (over y, z_hi, core).
Axes of the slice: x: 4, y: 8, z: 8 (z_hi: 2, z_lo: 4; z = z_hi * 4 + z_lo), core: 2. Of those that a mesh axis runs over, the one named last changes fastest.
Arguments:
- queries: bfloat16 [65536, 128], P(('outer', 'inner')), may hold values from -6 to 6
- keys: bfloat16 [65536, 128], P(('outer', 'inner')), may hold values from -6 to 6
- values: bfloat16 [65536, 128], P(('outer', 'inner')), may hold values from -6 to 6
- attended: bfloat16 [65536, 128], P(('outer', 'inner')), may hold values from -3 to 3
- out_grad: bfloat16 [65536, 128], P(('outer', 'inner')), may hold values from -384 to 384
- logsumexp: float32 [65536], P(('outer', 'inner')), may hold values from 10 to 11.5
Outputs:
- query_grad: bfloat16 [65536, 128], P(('outer', 'inner'))
- key_grad: bfloat16 [65536, 128], P(('outer', 'inner'))
- value_grad: bfloat16 [65536, 128], P(('outer', 'inner'))
The draws below stay inside these ranges and needn't reach their ends.
All inputs are finite; a program needn't handle non-finite values.
Results may differ from the reference program's by a relative error of at most 0.008.
Values may be sent and summed in bfloat16 or wider, within the bound.
A program may use at most 64 MiB of HBM per device.

```python
import jax
import jax.numpy as jnp
from jax import lax

HEAD = 128
SEQ = 65536


def block_levels(key, dims, shards, least, largest):
    loudness, own = 1.0, jax.random.fold_in(key, 6)
    for axis_at, shards_of in shards:
        heights = jnp.exp(jax.random.uniform(jax.random.fold_in(own, axis_at), (shards_of,), jnp.float32, least / len(shards), largest / len(shards)))
        loudness = loudness * jnp.repeat(heights, dims[axis_at] // shards_of).reshape([-1 if axis == axis_at else 1 for axis in range(len(dims))])
    return loudness


def gaussian(key, extent, scale, reach, split=(), kind=jnp.bfloat16):
    values = jax.random.normal(key, extent, jnp.float32) * scale
    if len(split) > 0:
        values = block_levels(key, extent, split, -0.22, 0.18) * values
    return jnp.clip(values, min=-reach, max=reach).astype(kind)


def setup_inputs(seed: int = 0) -> dict:
    seeds = jax.random.split(jax.random.key(seed), 7)
    return {
        "queries": gaussian(seeds[0], (SEQ, HEAD), 1.0, 6.0, ((0, 512),)),
        "keys": gaussian(seeds[1], (SEQ, HEAD), 1.0, 6.0, ((0, 512),)),
        "values": gaussian(seeds[2], (SEQ, HEAD), 1.0, 6.0, ((0, 512),)),
        "attended": gaussian(seeds[3], (SEQ, HEAD), 0.5, 3.0, ((0, 512),)),
        "out_grad": gaussian(seeds[4], (SEQ, HEAD), 64.0, 384.0, ((0, 512),)),
        "logsumexp": jnp.clip(10.0 + 1.5 * jax.random.uniform(seeds[5], (SEQ,), jnp.float32) ** block_levels(seeds[5], (SEQ,), ((0, 512),), -0.2, 0.2), 10.0, 11.5),
    }


def reference(queries, keys, values, attended, out_grad, logsumexp):
    scale = HEAD ** -0.5
    width = min(512, SEQ)
    count = SEQ // width
    delta = jnp.sum(out_grad.astype(jnp.float32) * attended.astype(jnp.float32), axis=1)
    query_blocks = queries.reshape(count, width, HEAD)
    grad_blocks = out_grad.reshape(count, width, HEAD)
    lse_blocks = logsumexp.reshape(count, width)
    delta_blocks = delta.reshape(count, width)

    def step(carry, block):
        key_acc, val_acc = carry
        qrow, grow, lrow, drow = block
        scores = jnp.dot(qrow, keys.T, preferred_element_type=jnp.float32) * scale
        probs = jnp.exp(scores - lrow[:, None])
        probs_low = probs.astype(jnp.bfloat16)
        prob_grad = jnp.dot(grow, values.T, preferred_element_type=jnp.float32)
        score_grad = (probs * (prob_grad - drow[:, None])).astype(jnp.bfloat16)
        query_part = (jnp.dot(score_grad, keys, preferred_element_type=jnp.float32) * scale).astype(jnp.bfloat16)
        key_acc = key_acc + jnp.dot(score_grad.T, qrow, preferred_element_type=jnp.float32) * scale
        val_acc = val_acc + jnp.dot(probs_low.T, grow, preferred_element_type=jnp.float32)
        return (key_acc, val_acc), query_part

    start = (jnp.zeros((SEQ, HEAD), jnp.float32), jnp.zeros((SEQ, HEAD), jnp.float32))
    (key_acc, val_acc), query_parts = lax.scan(step, start, (query_blocks, grad_blocks, lse_blocks, delta_blocks))
    query_grad = query_parts.reshape(SEQ, HEAD)
    return query_grad, key_acc.astype(jnp.bfloat16), val_acc.astype(jnp.bfloat16)
```

```python
import jax
import jax.numpy as jnp
from jax import lax
from jax.experimental import pallas as pl
from jax.experimental.pallas import tpu as pltpu
from jax.sharding import PartitionSpec as P

MESH = pl.DeviceIdType.MESH
F32, BF16 = jnp.float32, jnp.bfloat16
H = 128
QP, KP = 2 * H, 4 * H
LOG2E = 1.4426950408889634


def dot(a, b, over_a, over_b):
    return lax.dot_general(
        a, b, (((over_a,), (over_b,)), ((), ())), preferred_element_type=F32
    )


def thirds(row):
    high = row.astype(BF16).astype(F32)
    rest = row - high
    middle = rest.astype(BF16).astype(F32)
    return high, middle, rest - middle


def kernel(
    q_ref, k_ref, v_ref, a_ref, g_ref, l_ref,
    oq_ref, ok_ref, ov_ref,
    qg, qs, kg, dq, dk, dv, pb, db,
    q_out, q_in, q_mine, q_theirs,
    c_out, c_in, k_out, k_in, k_mine, k_theirs,
    send, recv,
):
    scale = H ** (-0.5)
    outer, inner = lax.axis_index("outer"), lax.axis_index("inner")
    x, z_lo = outer % 4, outer // 4
    y, z_hi, core = inner // 4, (inner // 2) % 2, inner % 2
    z = z_hi * 4 + z_lo

    def device(x, y, z, core):
        return ((z % 4) * 4 + x, y * 4 + (z // 4) * 2 + core)

    sibling = device(x, y, z, 1 - core)
    q_pair = device(x + 1 - 2 * (x % 2), y, z, core)
    k_pair = device(3 - x, y, z, core)
    z_ring = (device(x, y, (z + 1) % 8, core), device(x, y, (z + 7) % 8, core))
    y_ring = (device(x, (y + 1) % 8, z, core), device(x, (y + 7) % 8, z, core))

    barrier = pltpu.get_barrier_semaphore()
    for other in (sibling, q_pair, k_pair, *z_ring, *y_ring):
        pl.semaphore_signal(barrier, inc=1, device_id=other, device_id_type=MESH)

    copies = {}

    def start(name, src, dst, to):
        index = len(copies)
        copies[name] = pltpu.make_async_remote_copy(
            src_ref=src, dst_ref=dst, send_sem=send.at[index], recv_sem=recv.at[index],
            device_id=to, device_id_type=MESH,
        )
        copies[name].start()

    def arrived(*names):
        for name in names:
            copies[name].wait_recv()

    main = pl.ds(H, 2 * H)
    qg[0:H, H : 2 * H] = q_ref[...]
    qg[0:H, 2 * H : 3 * H] = g_ref[...]
    kg[0:H, H : 2 * H] = k_ref[...]
    kg[0:H, 2 * H : 3 * H] = v_ref[...]
    product = g_ref[...].astype(F32) * a_ref[...].astype(F32)
    delta = jnp.sum(product.T, axis=0, keepdims=True)
    line = lax.broadcasted_iota(jnp.int32, (16, H), 0)
    stats = jnp.zeros((16, H), F32)
    for at, row in enumerate((*thirds(l_ref[...] * (H**0.5)), *thirds(delta))):
        stats = jnp.where(line == at, row, stats)
    qs[0] = stats.astype(BF16)

    pl.semaphore_wait(barrier, 7)

    def send_queries(name, src, dst, block, count, to):
        rows = lambda slot: pl.ds(slot * QP + block * H, count * H)
        some = lambda slot: pl.ds(slot * 2 + block, count)
        start(name, qg.at[rows(src), main], qg.at[rows(dst), main], to)
        start(name + "s", qs.at[some(src)], qs.at[some(dst)], to)

    def send_keys(name, src, dst, block, count, to):
        rows = lambda slot: pl.ds(slot * KP + block * H, count * H)
        start(name, kg.at[rows(src), main], kg.at[rows(dst), main], to)

    def share_keys(name, slot, block, count):
        here = pl.ds(slot * KP + block * H, count * H)
        there = pl.ds(slot * KP + (2 + block) * H, count * H)
        start(name, kg.at[here, main], kg.at[there, main], sibling)

    here, there = pl.ds(0, H), pl.ds(H, H)
    start("qx", qg.at[here, main], qg.at[there, main], q_pair)
    start("qxs", qs.at[pl.ds(0, 1)], qs.at[pl.ds(1, 1)], q_pair)
    start("kx", kg.at[here, main], kg.at[there, main], k_pair)
    for way in range(2):
        send_queries(f"q1{way}a", 0, 1 + way, 0, 1, z_ring[way])
        send_keys(f"k1{way}a", 0, 1 + way, 0, 1, y_ring[way])
    share_keys("c0a", 0, 0, 1)

    lane = lax.broadcasted_iota(jnp.int32, (KP, H), 1)
    minus = jnp.where(lane < 3, -1.0, 0.0).astype(BF16)

    def clear(slot, _):
        rows = pl.ds(pl.multiple_of(slot * KP, KP), KP)
        kg[rows, 0:H] = minus
        kg[rows, 3 * H : 4 * H] = minus
        dk[:, rows] = jnp.zeros((H, KP), F32)
        dv[:, rows] = jnp.zeros((H, KP), F32)
        some = pl.ds(pl.multiple_of(slot * QP, QP), QP)
        dq[some, :] = jnp.zeros((QP, H), F32)

    lax.fori_loop(0, 8, clear, None)

    spread_at = lax.broadcasted_iota(jnp.int32, (16, H), 1)
    spread_l = jnp.where((line == spread_at) & (line < 3), 1.0, 0.0).astype(BF16)
    spread_d = jnp.where((line == spread_at + 3) & (line < 6), 1.0, 0.0).astype(BF16)

    def prepare(slot):
        for block in range(2):
            rows = pl.ds(slot * QP + block * H, H)
            these = qs[slot * 2 + block]
            qg[rows, 0:H] = dot(these, spread_l, 0, 0).astype(BF16)
            qg[rows, 3 * H : 4 * H] = dot(these, spread_d, 0, 0).astype(BF16)

    def tiles(first, count, columns):
        at, size = first * QP, count * QP
        rows = pl.ds(at, size)

        def one(slot):
            keys = pl.ds(pl.multiple_of(slot * KP, KP), KP)
            probs = jnp.exp2(dot(qg[rows, 0 : 2 * H], kg[keys, 0 : 2 * H], 1, 1) * (scale * LOG2E))
            shifted = dot(qg[rows, 2 * H : 4 * H], kg[keys, 2 * H : 4 * H], 1, 1)
            db[0:size] = (probs * shifted).astype(BF16)
            pb[0:size] = probs.astype(BF16)
            dv[:, keys] += dot(qg[rows, 2 * H : 3 * H], pb[0:size], 0, 0)
            dk[:, keys] += dot(qg[rows, H : 2 * H], db[0:size], 0, 0)
            dq[rows, :] += dot(db[0:size], kg[keys, H : 2 * H], 1, 0)

        low, high = columns
        if high - low == 1:
            one(low)
        else:
            lax.fori_loop(low, high, lambda slot, _: one(slot), None)

    arrived("qx", "qxs", "kx")
    for way in range(2):
        send_queries(f"q1{way}b", 0, 1 + way, 1, 1, z_ring[way])
        send_keys(f"k1{way}b", 0, 1 + way, 1, 1, y_ring[way])
    share_keys("c0b", 0, 1, 1)
    prepare(0)
    for way in range(2):
        arrived(f"q1{way}a", f"q1{way}as", f"q1{way}b", f"q1{way}bs")
        send_queries(f"q2{way}", 1 + way, 3 + way, 0, 2, z_ring[way])
        arrived(f"k1{way}a", f"k1{way}b")
        send_keys(f"k2{way}", 1 + way, 3 + way, 0, 2, y_ring[way])
        share_keys(f"c{1 + way}", 1 + way, 0, 2)
        prepare(1 + way)
    arrived("c0a", "c0b", "c1", "c2")
    tiles(0, 3, (0, 3))
    for way in range(2):
        arrived(f"q2{way}", f"q2{way}s")
        send_queries(f"q3{way}", 3 + way, 5 + way, 0, 2, z_ring[way])
        arrived(f"k2{way}")
        send_keys(f"k3{way}", 3 + way, 5 + way, 0, 2, y_ring[way])
        share_keys(f"c{3 + way}", 3 + way, 0, 2)
        prepare(3 + way)
    tiles(3, 2, (0, 3))
    arrived("c3", "c4")
    tiles(0, 5, (3, 4))
    for way in range(2):
        arrived(f"q3{way}", f"q3{way}s")
        send_queries(f"q4{way}", 5 + way, 7, way, 1, z_ring[way])
        arrived(f"k3{way}")
        send_keys(f"k4{way}", 5 + way, 7, way, 1, y_ring[way])
        share_keys(f"c{5 + way}", 5 + way, 0, 2)
        prepare(5 + way)
    tiles(0, 5, (4, 5))
    for way in range(2):
        arrived(f"q4{way}", f"q4{way}s", f"k4{way}")
    share_keys("c7", 7, 0, 2)
    prepare(7)

    def swap(slot):
        theirs = pl.ds(slot * KP + 2 * H, 2 * H)
        c_out[slot, 0] = dk[:, theirs].astype(BF16)
        c_out[slot, 1] = dv[:, theirs].astype(BF16)
        start(f"s{slot}", c_out.at[slot], c_in.at[slot], sibling)

    def mine(slot, which, grads, block, count):
        lanes = pl.ds(slot * KP + block * H, count * H)
        part = pl.ds(block * H, count * H)
        return grads[:, lanes] + c_in[slot, which, :, part].astype(F32)

    def pass_keys(step, way):
        slot = 10 - 2 * step - way
        if step == 1:
            part = pl.ds(way * H, H)
            for which, grads in enumerate((dk, dv)):
                k_out[way, 0, which, :, part] = mine(7, which, grads, way, 1).astype(BF16)
            start(
                f"ks1{way}", k_out.at[way, 0, :, :, part], k_in.at[way, 0, :, :, part], y_ring[way]
            )
            return
        arrived(f"ks{step - 1}{way}")
        for which, grads in enumerate((dk, dv)):
            for block in range(2):
                part = pl.ds(block * H, H)
                total = mine(slot, which, grads, block, 1)
                if step > 2 or block == way:
                    total += k_in[way, step - 2, which, :, part].astype(F32)
                k_out[way, step - 1, which, :, part] = total.astype(BF16)
        start(f"ks{step}{way}", k_out.at[way, step - 1], k_in.at[way, step - 1], y_ring[way])

    def pass_queries(step, way):
        slot = 10 - 2 * step - way
        if step == 1:
            part = pl.ds(way * H, H)
            q_out[way, 0, part] = dq[pl.ds(7 * QP + way * H, H), :].astype(BF16)
            start(f"qs1{way}", q_out.at[way, 0, part], q_in.at[way, 0, part], z_ring[way])
            return
        arrived(f"qs{step - 1}{way}")
        for block in range(2):
            part = pl.ds(block * H, H)
            total = dq[pl.ds(slot * QP + block * H, H), :]
            if step > 2 or block == way:
                total += q_in[way, step - 2, part].astype(F32)
            q_out[way, step - 1, part] = total.astype(BF16)
        start(f"qs{step}{way}", q_out.at[way, step - 1], q_in.at[way, step - 1], z_ring[way])

    arrived("c5", "c6", "c7")
    tiles(0, 8, (7, 8))
    swap(7)
    tiles(0, 8, (5, 6))
    swap(5)
    arrived("s7")
    pass_keys(1, 0)
    pass_keys(1, 1)
    tiles(0, 8, (6, 7))
    swap(6)
    tiles(5, 3, (3, 4))
    swap(3)
    arrived("s5", "s6")
    pass_keys(2, 0)
    pass_keys(2, 1)
    tiles(5, 3, (4, 5))
    swap(4)
    tiles(5, 3, (1, 3))
    swap(1)
    swap(2)
    tiles(5, 3, (0, 1))
    swap(0)
    for way in range(2):
        pass_queries(1, way)
    arrived("s3", "s4")
    for way in range(2):
        pass_keys(3, way)
    arrived("s0", "s1", "s2")
    for step in (2, 3, 4):
        for way in range(2):
            pass_queries(step, way)
        if step == 3:
            for way in range(2):
                pass_keys(4, way)

    arrived("qs40", "qs41")

    def own_queries(block):
        part = pl.ds(block * H, H)
        return dq[part, :] + q_in[0, 3, part].astype(F32) + q_in[1, 3, part].astype(F32)

    q_mine[...] = own_queries(1).astype(BF16)
    start("qp", q_mine, q_theirs, q_pair)

    def own_keys(which, grads, block):
        part = pl.ds(block * H, H)
        total = mine(0, which, grads, block, 1)
        for way in range(2):
            total += k_in[way, 3, which, :, part].astype(F32)
        return total

    arrived("ks40", "ks41")
    for which, grads in enumerate((dk, dv)):
        k_mine[which] = own_keys(which, grads, 1).astype(BF16)
    start("kp", k_mine, k_theirs, k_pair)
    arrived("qp")
    oq_ref[...] = ((own_queries(0) + q_theirs[...].astype(F32)) * scale).astype(BF16)
    arrived("kp")
    for which, (grads, out, by) in enumerate(((dk, ok_ref, scale), (dv, ov_ref, 1.0))):
        total = own_keys(which, grads, 0) + k_theirs[which].astype(F32)
        out[...] = (total * by).T.astype(BF16)
    for copy in copies.values():
        copy.wait_send()


COPIES = 96


def shards(queries, keys, values, attended, out_grad, logsumexp):
    vmem = pl.BlockSpec(memory_space=pltpu.VMEM)
    block = jax.ShapeDtypeStruct((H, H), BF16)
    return pl.pallas_call(
        kernel,
        out_shape=(block, block, block),
        in_specs=[vmem] * 6,
        out_specs=[vmem] * 3,
        scratch_shapes=[
            pltpu.VMEM((8 * QP, 4 * H), BF16),
            pltpu.VMEM((16, 16, H), BF16),
            pltpu.VMEM((8 * KP, 4 * H), BF16),
            pltpu.VMEM((8 * QP, H), F32),
            pltpu.VMEM((H, 8 * KP), F32),
            pltpu.VMEM((H, 8 * KP), F32),
            pltpu.VMEM((8 * QP, KP), BF16),
            pltpu.VMEM((8 * QP, KP), BF16),
            pltpu.VMEM((2, 4, QP, H), BF16),
            pltpu.VMEM((2, 4, QP, H), BF16),
            pltpu.VMEM((H, H), BF16),
            pltpu.VMEM((H, H), BF16),
            pltpu.VMEM((8, 2, H, 2 * H), BF16),
            pltpu.VMEM((8, 2, H, 2 * H), BF16),
            pltpu.VMEM((2, 4, 2, H, 2 * H), BF16),
            pltpu.VMEM((2, 4, 2, H, 2 * H), BF16),
            pltpu.VMEM((2, H, H), BF16),
            pltpu.VMEM((2, H, H), BF16),
            pltpu.SemaphoreType.DMA((COPIES,)),
            pltpu.SemaphoreType.DMA((COPIES,)),
        ],
        compiler_params=pltpu.CompilerParams(
            collective_id=0, has_side_effects=True, vmem_limit_bytes=56 * 2**20
        ),
    )(queries, keys, values, attended, out_grad, logsumexp.reshape(1, H))


def solution(mesh):
    rows, flat = P(("outer", "inner"), None), P(("outer", "inner"))
    return jax.shard_map(
        shards,
        mesh=mesh,
        in_specs=(rows, rows, rows, rows, rows, flat),
        out_specs=(rows, rows, rows),
        check_vma=False,
    )
```

```python
import jax
import jax.numpy as jnp
from jax import lax
from jax.experimental import pallas as pl
from jax.experimental.pallas import tpu as pltpu
from jax.sharding import PartitionSpec as P

MESH = pl.DeviceIdType.MESH
F32, BF16 = jnp.float32, jnp.bfloat16
H = 128
LEVEL = 4 * H
OFFSETS = (0, -1, 1, -2, 2, -3, 3, 4)
OWN = (0, 2, 3, 4, 5, 8, 9, 12)
PAIR = (1, 6, 7, 10, 11, 13, 14, 15)
LOG2E = 1.4426950408889634


def dot(a, b, over_a, over_b):
    return lax.dot_general(
        a, b, (((over_a,), (over_b,)), ((), ())), preferred_element_type=F32
    )


def thirds(row):
    high = row.astype(BF16).astype(F32)
    rest = row - high
    middle = rest.astype(BF16).astype(F32)
    return high, middle, rest - middle


def kernel(
    q_ref, k_ref, v_ref, a_ref, g_ref, l_ref,
    oq_ref, ok_ref, ov_ref,
    qg, qs, kg, dq, dk, dv, pb, db,
    c_out, c_in, kx_out, kx_in, k_out, k_in, qx_out, qx_in, q_out, q_in,
    send, recv,
):
    scale = H ** (-0.5)
    outer, inner = lax.axis_index("outer"), lax.axis_index("inner")
    x, z_lo = outer % 4, outer // 4
    y, z_hi, core = inner // 4, (inner // 2) % 2, inner % 2
    z = z_hi * 4 + z_lo

    def device(x, y, z, core):
        return ((z % 4) * 4 + x, y * 4 + (z // 4) * 2 + core)

    sibling = device(x, y, z, 1 - core)
    q_pair = device(x + 1 - 2 * (x % 2), y, z, core)
    k_pair = device(3 - x, y, z, core)

    def z_ring(offset):
        return device(x, y, (z + offset + 8) % 8, core)

    def y_ring(offset):
        return device(x, (y + offset + 8) % 8, z, core)

    barrier = pltpu.get_barrier_semaphore()
    others = [sibling, q_pair, k_pair]
    for offset in OFFSETS[1:]:
        others += [z_ring(offset), y_ring(offset)]
    for other in others:
        pl.semaphore_signal(barrier, inc=1, device_id=other, device_id_type=MESH)

    copies = {}

    def start(name, src, dst, to):
        index = len(copies)
        copies[name] = pltpu.make_async_remote_copy(
            src_ref=src, dst_ref=dst, send_sem=send.at[index], recv_sem=recv.at[index],
            device_id=to, device_id_type=MESH,
        )
        copies[name].start()

    def arrived(*names):
        for name in names:
            copies[name].wait_recv()

    main = pl.ds(H, 2 * H)
    qg[0:H, H : 2 * H] = q_ref[...]
    qg[0:H, 2 * H : 3 * H] = g_ref[...]
    kg[0:H, H : 2 * H] = k_ref[...]
    kg[0:H, 2 * H : 3 * H] = v_ref[...]
    product = g_ref[...].astype(F32) * a_ref[...].astype(F32)
    delta = jnp.sum(product.T, axis=0, keepdims=True)
    line = lax.broadcasted_iota(jnp.int32, (16, H), 0)
    stats = jnp.zeros((16, H), F32)
    for at, row in enumerate((*thirds(l_ref[...] * (H**0.5)), *thirds(delta))):
        stats = jnp.where(line == at, row, stats)
    qs[0] = stats.astype(BF16)

    pl.semaphore_wait(barrier, len(others))

    def key_rows(block, count):
        return pl.ds((block // 4) * 2 * LEVEL + (block % 4) * H, count * H)

    def send_queries(name, src, dst, count, to):
        start(
            name, qg.at[pl.ds(src * H, count * H), main], qg.at[pl.ds(dst * H, count * H), main], to
        )
        start(name + "s", qs.at[pl.ds(src, count)], qs.at[pl.ds(dst, count)], to)

    def send_keys(name, src, dst, count, to):
        start(name, kg.at[key_rows(src, count), main], kg.at[key_rows(dst, count), main], to)

    def share_keys(level):
        here, there = level * 2 * LEVEL, (level * 2 + 1) * LEVEL
        start(f"c{level}", kg.at[pl.ds(here, LEVEL), main], kg.at[pl.ds(there, LEVEL), main], sibling)

    def hand_on(slot, count):
        send_queries(f"qx{slot}", OWN[slot], PAIR[slot], count, q_pair)
        send_keys(f"kx{slot}", OWN[slot], PAIR[slot], count, k_pair)

    def came(*slots):
        for slot in slots:
            arrived(f"q{slot}", f"q{slot}s", f"k{slot}")

    def handed(*slots):
        for slot in slots:
            arrived(f"qx{slot}", f"qx{slot}s", f"kx{slot}")

    for slot in (1, 2):
        send_queries(f"q{slot}", 0, OWN[slot], 1, z_ring(-OFFSETS[slot]))
        send_keys(f"k{slot}", 0, OWN[slot], 1, y_ring(-OFFSETS[slot]))
    hand_on(0, 1)
    for slot in range(3, 8):
        send_queries(f"q{slot}", 0, OWN[slot], 1, z_ring(-OFFSETS[slot]))
        send_keys(f"k{slot}", 0, OWN[slot], 1, y_ring(-OFFSETS[slot]))

    lane = lax.broadcasted_iota(jnp.int32, (LEVEL, H), 1)
    minus = jnp.where(lane < 3, -1.0, 0.0).astype(BF16)

    def clear(column, _):
        rows = pl.ds(pl.multiple_of(column * LEVEL, LEVEL), LEVEL)
        kg[rows, 0:H] = minus
        kg[rows, 3 * H : 4 * H] = minus
        dk[:, rows] = jnp.zeros((H, LEVEL), F32)
        dv[:, rows] = jnp.zeros((H, LEVEL), F32)
        some = pl.ds(pl.multiple_of(column * 2 * H, 2 * H), 2 * H)
        dq[some, :] = jnp.zeros((2 * H, H), F32)

    lax.fori_loop(0, 8, clear, None)

    spread_at = lax.broadcasted_iota(jnp.int32, (16, H), 1)
    spread_l = jnp.where((line == spread_at) & (line < 3), 1.0, 0.0).astype(BF16)
    spread_d = jnp.where((line == spread_at + 3) & (line < 6), 1.0, 0.0).astype(BF16)

    def prepare(level):
        for block in range(4 * level, 4 * level + 4):
            rows = pl.ds(block * H, H)
            these = qs[block]
            qg[rows, 0:H] = dot(these, spread_l, 0, 0).astype(BF16)
            qg[rows, 3 * H : 4 * H] = dot(these, spread_d, 0, 0).astype(BF16)

    def tiles(first, count, *columns):
        size = count * LEVEL
        rows = pl.ds(first * LEVEL, size)

        def one(column):
            keys = pl.ds(pl.multiple_of(column * LEVEL, LEVEL), LEVEL)
            probs = jnp.exp2(dot(qg[rows, 0 : 2 * H], kg[keys, 0 : 2 * H], 1, 1) * (scale * LOG2E))
            shifted = dot(qg[rows, 2 * H : 4 * H], kg[keys, 2 * H : 4 * H], 1, 1)
            db[0:size] = (probs * shifted).astype(BF16)
            pb[0:size] = probs.astype(BF16)
            dv[:, keys] += dot(qg[rows, 2 * H : 3 * H], pb[0:size], 0, 0)
            dk[:, keys] += dot(qg[rows, H : 2 * H], db[0:size], 0, 0)
            dq[rows, :] += dot(db[0:size], kg[keys, H : 2 * H], 1, 0)

        if len(columns) == 1:
            one(columns[0])
        else:
            by = columns[1] - columns[0]
            lax.fori_loop(
                0, len(columns), lambda index, _: one(columns[0] + by * index), None
            )

    came(1, 2)
    hand_on(1, 2)
    handed(0)
    share_keys(0)
    prepare(0)
    tiles(0, 1, 0)
    came(3, 4)
    hand_on(3, 2)
    arrived("c0")
    tiles(0, 1, 1)
    handed(1)
    share_keys(1)
    prepare(1)
    tiles(1, 1, 0, 1)
    came(5, 6)
    hand_on(5, 2)
    arrived("c1")
    tiles(0, 2, 2, 3)
    came(7)
    hand_on(7, 1)
    handed(3)
    share_keys(2)
    prepare(2)
    arrived("c2")
    tiles(0, 2, 4, 5)
    handed(5, 7)
    share_keys(3)
    prepare(3)
    arrived("c3")

    def swap(level):
        theirs = pl.ds((2 * level + 1) * LEVEL, LEVEL)
        c_out[level, 0] = dk[:, theirs].astype(BF16)
        c_out[level, 1] = dv[:, theirs].astype(BF16)
        start(f"s{level}", c_out.at[level], c_in.at[level], sibling)

    def key_sum(which, block, count):
        grads = (dk, dv)[which]
        level, part = block // 4, pl.ds((block % 4) * H, count * H)
        here = pl.ds(level * 2 * LEVEL + (block % 4) * H, count * H)
        return grads[:, here] + c_in[level, which, :, part].astype(F32)

    def slots(first, count):
        return pl.ds(first * H, count * H)

    def keys_to_pair(first, count):
        part = slots(first, count)
        for which in range(2):
            kx_out[which, :, part] = key_sum(which, PAIR[first], count).astype(BF16)
        start(f"dkx{first}", kx_out.at[:, :, part], kx_in.at[:, :, part], k_pair)

    def key_total(which, slot):
        return key_sum(which, OWN[slot], 1) + kx_in[which, :, slots(slot, 1)].astype(F32)

    def keys_to_owner(slot):
        for which in range(2):
            k_out[slot, which] = key_total(which, slot).astype(BF16)
        start(f"dk{slot}", k_out.at[slot], k_in.at[slot], y_ring(OFFSETS[slot]))

    def queries_to_pair(first, count):
        part = slots(first, count)
        qx_out[part] = dq[slots(PAIR[first], count), :].astype(BF16)
        start(f"dqx{first}", qx_out.at[part], qx_in.at[part], q_pair)

    def query_total(slot):
        return dq[slots(OWN[slot], 1), :] + qx_in[slots(slot, 1)].astype(F32)

    def queries_to_owner(slot):
        q_out[slot] = query_total(slot).astype(BF16)
        start(f"dq{slot}", q_out.at[slot], q_in.at[slot], z_ring(OFFSETS[slot]))

    tiles(0, 4, 7)
    swap(3)
    tiles(0, 4, 6)
    arrived("s3")
    keys_to_pair(7, 1)
    keys_to_pair(5, 2)
    tiles(2, 2, 5)
    swap(2)
    queries_to_pair(1, 2)
    queries_to_pair(0, 1)
    tiles(2, 2, 4)
    arrived("s2")
    keys_to_pair(3, 2)
    tiles(3, 1, 3, 2)
    arrived("dkx7")
    keys_to_owner(7)
    tiles(3, 1, 1, 0)
    queries_to_pair(7, 1)
    queries_to_pair(5, 2)
    arrived("dkx5")
    keys_to_owner(5)
    keys_to_owner(6)
    arrived("dqx0", "dqx1")
    queries_to_owner(1)
    queries_to_owner(2)
    tiles(2, 1, 3)
    swap(1)
    tiles(2, 1, 2)
    arrived("s1")
    keys_to_pair(1, 2)
    tiles(2, 1, 1)
    swap(0)
    arrived("dkx3")
    keys_to_owner(3)
    keys_to_owner(4)
    tiles(2, 1, 0)
    queries_to_pair(3, 2)
    arrived("dqx7")
    queries_to_owner(7)
    arrived("dqx5")
    queries_to_owner(5)
    queries_to_owner(6)
    arrived("s0")
    keys_to_pair(0, 1)
    arrived("dkx1")
    keys_to_owner(1)
    keys_to_owner(2)
    arrived("dqx3")
    queries_to_owner(3)
    queries_to_owner(4)

    total = query_total(0)
    for slot in (1, 2, 7, 5, 6, 3, 4):
        arrived(f"dq{slot}")
        total += q_in[slot].astype(F32)
    oq_ref[...] = (total * scale).astype(BF16)
    arrived("dkx0")
    for slot in (7, 5, 6, 3, 4, 1, 2):
        arrived(f"dk{slot}")
    for which, (out, by) in enumerate(((ok_ref, scale), (ov_ref, 1.0))):
        total = key_total(which, 0)
        for slot in range(1, 8):
            total += k_in[slot, which].astype(F32)
        out[...] = (total * by).T.astype(BF16)
    for copy in copies.values():
        copy.wait_send()


COPIES = 80


def shards(queries, keys, values, attended, out_grad, logsumexp):
    vmem = pl.BlockSpec(memory_space=pltpu.VMEM)
    block = jax.ShapeDtypeStruct((H, H), BF16)
    keys_shape = pltpu.VMEM((2, H, 8 * H), BF16)
    return pl.pallas_call(
        kernel,
        out_shape=(block, block, block),
        in_specs=[vmem] * 6,
        out_specs=[vmem] * 3,
        scratch_shapes=[
            pltpu.VMEM((4 * LEVEL, 4 * H), BF16),
            pltpu.VMEM((16, 16, H), BF16),
            pltpu.VMEM((8 * LEVEL, 4 * H), BF16),
            pltpu.VMEM((4 * LEVEL, H), F32),
            pltpu.VMEM((H, 8 * LEVEL), F32),
            pltpu.VMEM((H, 8 * LEVEL), F32),
            pltpu.VMEM((4 * LEVEL, LEVEL), BF16),
            pltpu.VMEM((4 * LEVEL, LEVEL), BF16),
            pltpu.VMEM((4, 2, H, LEVEL), BF16),
            pltpu.VMEM((4, 2, H, LEVEL), BF16),
            keys_shape,
            keys_shape,
            pltpu.VMEM((8, 2, H, H), BF16),
            pltpu.VMEM((8, 2, H, H), BF16),
            pltpu.VMEM((8 * H, H), BF16),
            pltpu.VMEM((8 * H, H), BF16),
            pltpu.VMEM((8, H, H), BF16),
            pltpu.VMEM((8, H, H), BF16),
            pltpu.SemaphoreType.DMA((COPIES,)),
            pltpu.SemaphoreType.DMA((COPIES,)),
        ],
        compiler_params=pltpu.CompilerParams(
            collective_id=0, has_side_effects=True, vmem_limit_bytes=56 * 2**20
        ),
    )(queries, keys, values, attended, out_grad, logsumexp.reshape(1, H))


def solution(mesh):
    rows, flat = P(("outer", "inner"), None), P(("outer", "inner"))
    return jax.shard_map(
        shards,
        mesh=mesh,
        in_specs=(rows, rows, rows, rows, rows, flat),
        out_specs=(rows, rows, rows),
        check_vma=False,
    )
```

```python
import jax
import jax.numpy as jnp
from jax import lax
from jax.experimental import pallas as pl
from jax.experimental.pallas import tpu as pltpu
from jax.sharding import PartitionSpec as P

MESH = pl.DeviceIdType.MESH
F32, BF16 = jnp.float32, jnp.bfloat16
H = 128
LEVEL = 4 * H
OFFSETS = (0, -1, 1, -2, 2, -3, 3, 4)
OWN = (0, 2, 3, 4, 5, 8, 9, 12)
PAIR = (1, 6, 7, 10, 11, 13, 14, 15)
LOG2E = 1.4426950408889634


def dot(a, b, over_a, over_b):
    return lax.dot_general(
        a, b, (((over_a,), (over_b,)), ((), ())), preferred_element_type=F32
    )


def thirds(row):
    high = row.astype(BF16).astype(F32)
    rest = row - high
    middle = rest.astype(BF16).astype(F32)
    return high, middle, rest - middle


def kernel(
    q_ref, k_ref, v_ref, a_ref, g_ref, l_ref,
    oq_ref, ok_ref, ov_ref,
    qg, qs, kg, dq, dk, dv, pb, db,
    c_out, c_in, kx_out, kx_in, k_out, k_in, qx_out, qx_in, q_out, q_in,
    send, recv,
):
    scale = H ** (-0.5)
    outer, inner = lax.axis_index("outer"), lax.axis_index("inner")
    x, z_lo = outer % 4, outer // 4
    y, z_hi, core = inner // 4, (inner // 2) % 2, inner % 2
    z = z_hi * 4 + z_lo

    def device(x, y, z, core):
        return ((z % 4) * 4 + x, y * 4 + (z // 4) * 2 + core)

    sibling = device(x, y, z, 1 - core)
    q_pair = device(x + 1 - 2 * (x % 2), y, z, core)
    k_pair = device(3 - x, y, z, core)

    def z_ring(offset):
        return device(x, y, (z + offset + 8) % 8, core)

    def y_ring(offset):
        return device(x, (y + offset + 8) % 8, z, core)

    barrier = pltpu.get_barrier_semaphore()
    others = [sibling, q_pair, k_pair]
    others += [z_ring(offset) for offset in OFFSETS[1:]]
    others += [y_ring(offset) for offset in OFFSETS[1:5]]
    for other in others:
        pl.semaphore_signal(barrier, inc=1, device_id=other, device_id_type=MESH)

    copies = {}

    def start(name, src, dst, to):
        index = len(copies)
        copies[name] = pltpu.make_async_remote_copy(
            src_ref=src, dst_ref=dst, send_sem=send.at[index], recv_sem=recv.at[index],
            device_id=to, device_id_type=MESH,
        )
        copies[name].start()

    def arrived(*names):
        for name in names:
            copies[name].wait_recv()

    main = pl.ds(H, 2 * H)
    qg[0:H, H : 2 * H] = q_ref[...]
    qg[0:H, 2 * H : 3 * H] = g_ref[...]
    kg[0:H, H : 2 * H] = k_ref[...]
    kg[0:H, 2 * H : 3 * H] = v_ref[...]
    product = g_ref[...].astype(F32) * a_ref[...].astype(F32)
    delta = jnp.sum(product.T, axis=0, keepdims=True)
    line = lax.broadcasted_iota(jnp.int32, (16, H), 0)
    stats = jnp.zeros((16, H), F32)
    for at, row in enumerate((*thirds(l_ref[...] * (H**0.5)), *thirds(delta))):
        stats = jnp.where(line == at, row, stats)
    qs[0] = stats.astype(BF16)

    pl.semaphore_wait(barrier, len(others))

    def key_rows(block, count):
        return pl.ds((block // 4) * 2 * LEVEL + (block % 4) * H, count * H)

    def send_queries(name, src, dst, count, to):
        start(
            name, qg.at[pl.ds(src * H, count * H), main], qg.at[pl.ds(dst * H, count * H), main], to
        )
        start(name + "s", qs.at[pl.ds(src, count)], qs.at[pl.ds(dst, count)], to)

    def send_keys(name, src, dst, count, to):
        start(name, kg.at[key_rows(src, count), main], kg.at[key_rows(dst, count), main], to)

    def share_keys(level):
        here, there = level * 2 * LEVEL, (level * 2 + 1) * LEVEL
        start(f"c{level}", kg.at[pl.ds(here, LEVEL), main], kg.at[pl.ds(there, LEVEL), main], sibling)

    def hand_on(slot, count):
        send_queries(f"qx{slot}", OWN[slot], PAIR[slot], count, q_pair)
        send_keys(f"kx{slot}", OWN[slot], PAIR[slot], count, k_pair)

    def send_on(slot, way):
        send_queries(f"q{slot + 2}", OWN[slot], OWN[slot + 2], 1, z_ring(way))
        send_keys(f"k{slot + 2}", OWN[slot], OWN[slot + 2], 1, y_ring(way))
        half = H // 2
        low = 0 if way > 0 else half
        there = pl.ds(OWN[7] * H + low, half)
        start(f"q7{way}", qg.at[pl.ds(OWN[slot] * H + low, half), main], qg.at[there, main], z_ring(2 * way))
        if way > 0:
            start("q7s", qs.at[pl.ds(OWN[slot], 1)], qs.at[pl.ds(OWN[7], 1)], z_ring(2))
        here, there = key_rows(OWN[slot], 1).start + low, key_rows(OWN[7], 1).start + low
        start(f"k7{way}", kg.at[pl.ds(here, half), main], kg.at[pl.ds(there, half), main], y_ring(2 * way))

    def came(*slots):
        for slot in slots:
            arrived(f"q{slot}", f"q{slot}s", f"k{slot}")

    def handed(*slots):
        for slot in slots:
            arrived(f"qx{slot}", f"qx{slot}s", f"kx{slot}")

    for slot in (1, 2):
        send_queries(f"q{slot}", 0, OWN[slot], 1, z_ring(-OFFSETS[slot]))
        send_keys(f"k{slot}", 0, OWN[slot], 1, y_ring(-OFFSETS[slot]))
    hand_on(0, 1)
    for slot in (3, 4):
        send_queries(f"q{slot}", 0, OWN[slot], 1, z_ring(-OFFSETS[slot]))
        send_keys(f"k{slot}", 0, OWN[slot], 1, y_ring(-OFFSETS[slot]))

    lane = lax.broadcasted_iota(jnp.int32, (LEVEL, H), 1)
    minus = jnp.where(lane < 3, -1.0, 0.0).astype(BF16)

    def clear(column, _):
        rows = pl.ds(pl.multiple_of(column * LEVEL, LEVEL), LEVEL)
        kg[rows, 0:H] = minus
        kg[rows, 3 * H : 4 * H] = minus
        dk[:, rows] = jnp.zeros((H, LEVEL), F32)
        dv[:, rows] = jnp.zeros((H, LEVEL), F32)
        some = pl.ds(pl.multiple_of(column * 2 * H, 2 * H), 2 * H)
        dq[some, :] = jnp.zeros((2 * H, H), F32)

    lax.fori_loop(0, 8, clear, None)

    spread_at = lax.broadcasted_iota(jnp.int32, (16, H), 1)
    spread_l = jnp.where((line == spread_at) & (line < 3), 1.0, 0.0).astype(BF16)
    spread_d = jnp.where((line == spread_at + 3) & (line < 6), 1.0, 0.0).astype(BF16)

    def prepare(level):
        for block in range(4 * level, 4 * level + 4):
            rows = pl.ds(block * H, H)
            these = qs[block]
            qg[rows, 0:H] = dot(these, spread_l, 0, 0).astype(BF16)
            qg[rows, 3 * H : 4 * H] = dot(these, spread_d, 0, 0).astype(BF16)

    def tiles(first, count, *columns):
        size = count * LEVEL
        rows = pl.ds(first * LEVEL, size)

        def one(column):
            keys = pl.ds(pl.multiple_of(column * LEVEL, LEVEL), LEVEL)
            probs = jnp.exp2(dot(qg[rows, 0 : 2 * H], kg[keys, 0 : 2 * H], 1, 1) * (scale * LOG2E))
            shifted = dot(qg[rows, 2 * H : 4 * H], kg[keys, 2 * H : 4 * H], 1, 1)
            db[0:size] = (probs * shifted).astype(BF16)
            pb[0:size] = probs.astype(BF16)
            dv[:, keys] += dot(qg[rows, 2 * H : 3 * H], pb[0:size], 0, 0)
            dk[:, keys] += dot(qg[rows, H : 2 * H], db[0:size], 0, 0)
            dq[rows, :] += dot(db[0:size], kg[keys, H : 2 * H], 1, 0)

        if len(columns) == 1:
            one(columns[0])
        else:
            by = columns[1] - columns[0]
            lax.fori_loop(
                0, len(columns), lambda index, _: one(columns[0] + by * index), None
            )

    came(1, 2)
    hand_on(1, 2)
    handed(0)
    share_keys(0)
    prepare(0)
    tiles(0, 1, 0)
    came(3, 4)
    send_on(3, 1)
    send_on(4, -1)
    hand_on(3, 2)
    arrived("c0")
    tiles(0, 1, 1)
    handed(1)
    share_keys(1)
    prepare(1)
    tiles(1, 1, 0, 1)
    came(5, 6)
    hand_on(5, 2)
    handed(3)
    share_keys(2)
    prepare(2)
    arrived("c1")
    tiles(0, 2, 2)
    arrived("q71", "q7-1", "q7s", "k71", "k7-1")
    hand_on(7, 1)
    tiles(0, 2, 3)
    arrived("c2")
    tiles(0, 3, 4, 5)
    handed(5, 7)
    share_keys(3)
    prepare(3)
    tiles(2, 1, 0, 1, 2, 3)
    arrived("c3")

    def swap(level):
        theirs = pl.ds((2 * level + 1) * LEVEL, LEVEL)
        c_out[level, 0] = dk[:, theirs].astype(BF16)
        c_out[level, 1] = dv[:, theirs].astype(BF16)
        start(f"s{level}", c_out.at[level], c_in.at[level], sibling)

    def key_sum(which, block, count):
        grads = (dk, dv)[which]
        level, part = block // 4, pl.ds((block % 4) * H, count * H)
        here = pl.ds(level * 2 * LEVEL + (block % 4) * H, count * H)
        return grads[:, here] + c_in[level, which, :, part].astype(F32)

    def slots(first, count):
        return pl.ds(first * H, count * H)

    def keys_to_pair(first, count):
        part = slots(first, count)
        for which in range(2):
            kx_out[which, :, part] = key_sum(which, PAIR[first], count).astype(BF16)
        start(f"dkx{first}", kx_out.at[:, :, part], kx_in.at[:, :, part], k_pair)

    def key_total(which, slot):
        total = key_sum(which, OWN[slot], 1) + kx_in[which, :, slots(slot, 1)].astype(F32)
        if slot in (3, 4):
            total += k_in[slot + 2, which].astype(F32)
            if which == 4 - slot:
                total += k_in[7, which].astype(F32)
        return total

    def keys_to_owner(slot):
        for which in range(2):
            k_out[slot, which] = key_total(which, slot).astype(BF16)
        if slot == 7:
            for which, to in enumerate((2, -2)):
                start(f"dk7{which}", k_out.at[7, which], k_in.at[7, which], y_ring(to))
        else:
            to = {5: -1, 6: 1}.get(slot, OFFSETS[slot])
            start(f"dk{slot}", k_out.at[slot], k_in.at[slot], y_ring(to))

    def queries_to_pair(first, count):
        part = slots(first, count)
        qx_out[part] = dq[slots(PAIR[first], count), :].astype(BF16)
        start(f"dqx{first}", qx_out.at[part], qx_in.at[part], q_pair)

    def query_total(slot):
        return dq[slots(OWN[slot], 1), :] + qx_in[slots(slot, 1)].astype(F32)

    def queries_to_owner(slot):
        q_out[slot] = query_total(slot).astype(BF16)
        start(f"dq{slot}", q_out.at[slot], q_in.at[slot], z_ring(OFFSETS[slot]))

    tiles(0, 4, 7)
    swap(3)
    tiles(0, 4, 6)
    arrived("s3")
    keys_to_pair(7, 1)
    keys_to_pair(5, 2)
    queries_to_pair(1, 2)
    queries_to_pair(0, 1)
    queries_to_pair(3, 2)
    tiles(3, 1, 5)
    swap(2)
    tiles(3, 1, 4)
    arrived("s2")
    keys_to_pair(3, 2)
    tiles(3, 1, 3)
    swap(1)
    tiles(3, 1, 2)
    arrived("s1")
    keys_to_pair(1, 2)
    arrived("dkx7")
    keys_to_owner(7)
    arrived("dkx5")
    keys_to_owner(5)
    keys_to_owner(6)
    tiles(3, 1, 1)
    swap(0)
    arrived("dqx0", "dqx1", "dqx3")
    for slot in range(1, 5):
        queries_to_owner(slot)
    tiles(3, 1, 0)
    queries_to_pair(7, 1)
    queries_to_pair(5, 2)
    arrived("s0")
    keys_to_pair(0, 1)
    arrived("dkx3", "dk70", "dk71", "dk5", "dk6")
    keys_to_owner(3)
    keys_to_owner(4)
    arrived("dkx1")
    keys_to_owner(1)
    keys_to_owner(2)
    arrived("dqx7")
    queries_to_owner(7)
    arrived("dqx5")
    queries_to_owner(5)
    queries_to_owner(6)

    total = query_total(0)
    for slot in range(1, 8):
        arrived(f"dq{slot}")
        total += q_in[slot].astype(F32)
    oq_ref[...] = (total * scale).astype(BF16)
    arrived("dkx0")
    arrived("dk3", "dk4", "dk1", "dk2")
    for which, (out, by) in enumerate(((ok_ref, scale), (ov_ref, 1.0))):
        total = key_total(which, 0)
        for slot in range(1, 5):
            total += k_in[slot, which].astype(F32)
        out[...] = (total * by).T.astype(BF16)
    for copy in copies.values():
        copy.wait_send()


COPIES = 80


def shards(queries, keys, values, attended, out_grad, logsumexp):
    vmem = pl.BlockSpec(memory_space=pltpu.VMEM)
    block = jax.ShapeDtypeStruct((H, H), BF16)
    keys_shape = pltpu.VMEM((2, H, 8 * H), BF16)
    return pl.pallas_call(
        kernel,
        out_shape=(block, block, block),
        in_specs=[vmem] * 6,
        out_specs=[vmem] * 3,
        scratch_shapes=[
            pltpu.VMEM((4 * LEVEL, 4 * H), BF16),
            pltpu.VMEM((16, 16, H), BF16),
            pltpu.VMEM((8 * LEVEL, 4 * H), BF16),
            pltpu.VMEM((4 * LEVEL, H), F32),
            pltpu.VMEM((H, 8 * LEVEL), F32),
            pltpu.VMEM((H, 8 * LEVEL), F32),
            pltpu.VMEM((4 * LEVEL, LEVEL), BF16),
            pltpu.VMEM((4 * LEVEL, LEVEL), BF16),
            pltpu.VMEM((4, 2, H, LEVEL), BF16),
            pltpu.VMEM((4, 2, H, LEVEL), BF16),
            keys_shape,
            keys_shape,
            pltpu.VMEM((8, 2, H, H), BF16),
            pltpu.VMEM((8, 2, H, H), BF16),
            pltpu.VMEM((8 * H, H), BF16),
            pltpu.VMEM((8 * H, H), BF16),
            pltpu.VMEM((8, H, H), BF16),
            pltpu.VMEM((8, H, H), BF16),
            pltpu.SemaphoreType.DMA((COPIES,)),
            pltpu.SemaphoreType.DMA((COPIES,)),
        ],
        compiler_params=pltpu.CompilerParams(
            collective_id=0, has_side_effects=True, vmem_limit_bytes=56 * 2**20
        ),
    )(queries, keys, values, attended, out_grad, logsumexp.reshape(1, H))


def solution(mesh):
    rows, flat = P(("outer", "inner"), None), P(("outer", "inner"))
    return jax.shard_map(
        shards,
        mesh=mesh,
        in_specs=(rows, rows, rows, rows, rows, flat),
        out_specs=(rows, rows, rows),
        check_vma=False,
    )
```

```python
import jax
import jax.numpy as jnp
from jax import lax
from jax.experimental import pallas as pl
from jax.experimental.pallas import tpu as pltpu
from jax.sharding import PartitionSpec as P

MESH = pl.DeviceIdType.MESH
F32, BF16 = jnp.float32, jnp.bfloat16
H = 128
LEVEL = 4 * H
OFFSETS = (0, -1, 1, -2, 2, -3, 3, 4)
OWN = (0, 2, 3, 4, 5, 8, 9, 12)
PAIR = (1, 6, 7, 10, 11, 13, 14, 15)
LOG2E = 1.4426950408889634


def dot(a, b, over_a, over_b):
    return lax.dot_general(
        a, b, (((over_a,), (over_b,)), ((), ())), preferred_element_type=F32
    )


def thirds(row):
    high = row.astype(BF16).astype(F32)
    rest = row - high
    middle = rest.astype(BF16).astype(F32)
    return high, middle, rest - middle


def kernel(
    q_ref, k_ref, v_ref, a_ref, g_ref, l_ref,
    out_ref,
    own_a, own_l, load, pw, dw,
    qg, qs, kg, dq, dk, dv, pb, db,
    c_out, c_in, kx_out, kx_in, k_out, k_in, qx_out, qx_in, q_out, q_in,
    send, recv,
):
    scale = H ** (-0.5)
    outer, inner = lax.axis_index("outer"), lax.axis_index("inner")
    x, z_lo = outer % 4, outer // 4
    y, z_hi, core = inner // 4, (inner // 2) % 2, inner % 2
    z = z_hi * 4 + z_lo

    def device(x, y, z, core):
        return ((z % 4) * 4 + x, y * 4 + (z // 4) * 2 + core)

    sibling = device(x, y, z, 1 - core)
    q_pair = device(x + 1 - 2 * (x % 2), y, z, core)
    k_pair = device(3 - x, y, z, core)

    def z_ring(offset):
        return device(x, y, (z + offset + 8) % 8, core)

    def y_ring(offset):
        return device(x, (y + offset + 8) % 8, z, core)

    barrier = pltpu.get_barrier_semaphore()
    others = [sibling, q_pair, k_pair]
    others += [z_ring(offset) for offset in OFFSETS[1:]]
    others += [y_ring(offset) for offset in OFFSETS[1:7]]
    for other in others:
        pl.semaphore_signal(barrier, inc=1, device_id=other, device_id_type=MESH)

    copies = {}

    def start(name, src, dst, to):
        index = len(copies)
        copies[name] = pltpu.make_async_remote_copy(
            src_ref=src, dst_ref=dst, send_sem=send.at[index], recv_sem=recv.at[index],
            device_id=to, device_id_type=MESH,
        )
        copies[name].start()

    def arrived(*names):
        for name in names:
            copies[name].wait_recv()

    main = pl.ds(H, 2 * H)
    mine, low, high = pl.ds(0, H), pl.ds(H, H), pl.ds(2 * H, H)
    loads = [
        pltpu.make_async_copy(src, dst, load.at[index])
        for index, (src, dst) in enumerate(
            (
                (q_ref, qg.at[mine, low]), (g_ref, qg.at[mine, high]), (k_ref, kg.at[mine, low]),
                (v_ref, kg.at[mine, high]), (a_ref, own_a), (l_ref, own_l),
            )
        )
    ]
    for copy in loads:
        copy.start()
    for copy in loads:
        copy.wait()
    pl.semaphore_wait(barrier, len(others))

    def key_rows(block, count):
        return pl.ds((block // 4) * 2 * LEVEL + (block % 4) * H, count * H)

    def send_rows(name, src, dst, count, to):
        start(
            name, qg.at[pl.ds(src * H, count * H), main], qg.at[pl.ds(dst * H, count * H), main], to
        )

    def send_stats(name, src, dst, count, to):
        start(name + "s", qs.at[pl.ds(src, count)], qs.at[pl.ds(dst, count)], to)

    def send_keys(name, src, dst, count, to):
        start(name, kg.at[key_rows(src, count), main], kg.at[key_rows(dst, count), main], to)

    def share_keys(level):
        here, there = level * 2 * LEVEL, (level * 2 + 1) * LEVEL
        start(f"c{level}", kg.at[pl.ds(here, LEVEL), main], kg.at[pl.ds(there, LEVEL), main], sibling)

    def hand_on(slot, count):
        send_rows(f"qx{slot}", OWN[slot], PAIR[slot], count, q_pair)
        send_keys(f"kx{slot}", OWN[slot], PAIR[slot], count, k_pair)

    def send_on(slot, way):
        send_rows(f"q{slot + 2}", OWN[slot], OWN[slot + 2], 1, z_ring(way))
        send_keys(f"k{slot + 2}", OWN[slot], OWN[slot + 2], 1, y_ring(way))
        half = H // 2
        low = 0 if way > 0 else half
        there = pl.ds(OWN[7] * H + low, half)
        start(f"q7{way}", qg.at[pl.ds(OWN[slot] * H + low, half), main], qg.at[there, main], z_ring(2 * way))
        here, there = key_rows(OWN[slot], 1).start + low, key_rows(OWN[7], 1).start + low
        start(f"k7{way}", kg.at[pl.ds(here, half), main], kg.at[pl.ds(there, half), main], y_ring(2 * way))

    def hand_stats(slot, count):
        arrived(*(f"q{slot + index}s" for index in range(count)))
        send_stats(f"qx{slot}", OWN[slot], PAIR[slot], count, q_pair)

    def came(*slots):
        for slot in slots:
            arrived(f"q{slot}", f"k{slot}")

    def handed(*slots):
        for slot in slots:
            arrived(f"qx{slot}", f"kx{slot}")

    def to_ring(slot):
        send_rows(f"q{slot}", 0, OWN[slot], 1, z_ring(-OFFSETS[slot]))
        send_keys(f"k{slot}", 0, OWN[slot], 1, y_ring(-OFFSETS[slot]))

    to_ring(1)
    to_ring(2)
    send_rows("qx0", 0, PAIR[0], 1, q_pair)
    send_keys("kx0", 0, PAIR[0], 1, k_pair)
    to_ring(3)
    to_ring(4)

    product = qg[mine, high].astype(F32) * own_a[...].astype(F32)
    delta = jnp.sum(product.T, axis=0, keepdims=True)
    line = lax.broadcasted_iota(jnp.int32, (16, H), 0)
    stats = jnp.zeros((16, H), F32)
    for at, row in enumerate((*thirds(own_l[...] * (H**0.5)), *thirds(delta))):
        stats = jnp.where(line == at, row, stats)
    qs[0] = stats.astype(BF16)
    for slot in range(1, 8):
        send_stats(f"q{slot}", 0, OWN[slot], 1, z_ring(-OFFSETS[slot]))
    send_stats("qx0", 0, PAIR[0], 1, q_pair)

    lane = lax.broadcasted_iota(jnp.int32, (LEVEL, H), 1)
    minus = jnp.where(lane < 3, -1.0, 0.0).astype(BF16)

    def clear(column, _):
        rows = pl.ds(pl.multiple_of(column * LEVEL, LEVEL), LEVEL)
        kg[rows, 0:H] = minus
        kg[rows, 3 * H : 4 * H] = minus
        dk[:, rows] = jnp.zeros((H, LEVEL), F32)
        dv[:, rows] = jnp.zeros((H, LEVEL), F32)
        some = pl.ds(pl.multiple_of(column * 2 * H, 2 * H), 2 * H)
        dq[some, :] = jnp.zeros((2 * H, H), F32)

    lax.fori_loop(0, 8, clear, None)

    spread_at = lax.broadcasted_iota(jnp.int32, (16, H), 1)
    spread_l = jnp.where((line == spread_at) & (line < 3), 1.0, 0.0).astype(BF16)
    spread_d = jnp.where((line == spread_at + 3) & (line < 6), 1.0, 0.0).astype(BF16)

    def prepare(level):
        for block in range(4 * level, 4 * level + 4):
            rows = pl.ds(block * H, H)
            these = qs[block]
            qg[rows, 0:H] = dot(these, spread_l, 0, 0).astype(BF16)
            qg[rows, 3 * H : 4 * H] = dot(these, spread_d, 0, 0).astype(BF16)

    def grads_of(rows, keys, p, d):
        probs = jnp.exp2(dot(qg[rows, 0 : 2 * H], kg[keys, 0 : 2 * H], 1, 1) * (scale * LOG2E))
        shifted = dot(qg[rows, 2 * H : 4 * H], kg[keys, 2 * H : 4 * H], 1, 1)
        d[...] = (probs * shifted).astype(BF16)
        p[...] = probs.astype(BF16)
        dv[:, keys] += dot(qg[rows, 2 * H : 3 * H], p[...], 0, 0)
        dk[:, keys] += dot(qg[rows, H : 2 * H], d[...], 0, 0)
        dq[rows, :] += dot(d[...], kg[keys, H : 2 * H], 1, 0)

    def tiles(first, count, column):
        size = pl.ds(0, count * LEVEL)
        rows, keys = pl.ds(first * LEVEL, count * LEVEL), pl.ds(column * LEVEL, LEVEL)
        grads_of(rows, keys, pb.at[size], db.at[size])

    def wide(first, level):
        grads_of(pl.ds(first * LEVEL, LEVEL), pl.ds(level * 2 * LEVEL, 2 * LEVEL), pw, dw)

    came(1, 2)
    hand_on(1, 2)
    hand_stats(1, 2)
    handed(0)
    share_keys(0)
    arrived("qx0s")
    prepare(0)
    tiles(0, 1, 0)
    came(3, 4)
    send_on(3, 1)
    send_on(4, -1)
    hand_on(3, 2)
    hand_stats(3, 2)
    arrived("c0")
    tiles(0, 1, 1)
    handed(1)
    share_keys(1)
    arrived("qx1s")
    prepare(1)
    hand_stats(5, 2)
    hand_stats(7, 1)
    wide(1, 0)
    came(5, 6)
    hand_on(5, 2)
    arrived("q71", "q7-1", "k71", "k7-1")
    hand_on(7, 1)
    tiles(0, 2, 2)
    arrived("c1")
    tiles(0, 2, 3)
    handed(3)
    share_keys(2)
    arrived("qx3s")
    prepare(2)
    tiles(0, 3, 4)
    arrived("c2")
    tiles(0, 3, 5)
    handed(5, 7)
    share_keys(3)
    arrived("qx5s", "qx7s")
    prepare(3)
    wide(2, 1)

    def swap(level):
        theirs = pl.ds((2 * level + 1) * LEVEL, LEVEL)
        c_out[level, 0] = dk[:, theirs].astype(BF16)
        c_out[level, 1] = dv[:, theirs].astype(BF16)
        start(f"s{level}", c_out.at[level], c_in.at[level], sibling)

    def key_sum(which, block, count):
        grads = (dk, dv)[which]
        level, part = block // 4, pl.ds((block % 4) * H, count * H)
        here = pl.ds(level * 2 * LEVEL + (block % 4) * H, count * H)
        return grads[:, here] + c_in[level, which, :, part].astype(F32)

    def slots(first, count):
        return pl.ds(first * H, count * H)

    def keys_to_pair(first, count):
        part = slots(first, count)
        for which in range(2):
            kx_out[which, :, part] = key_sum(which, PAIR[first], count).astype(BF16)
        start(f"dkx{first}", kx_out.at[:, :, part], kx_in.at[:, :, part], k_pair)

    def key_total(which, slot):
        total = key_sum(which, OWN[slot], 1) + kx_in[which, :, slots(slot, 1)].astype(F32)
        if slot in (3, 4) and which == 4 - slot:
            total += k_in[7, which].astype(F32)
        return total

    def keys_to_owner(slot):
        for which in range(2):
            k_out[slot, which] = key_total(which, slot).astype(BF16)
        if slot == 7:
            for which, to in enumerate((2, -2)):
                start(f"dk7{which}", k_out.at[7, which], k_in.at[7, which], y_ring(to))
        else:
            start(f"dk{slot}", k_out.at[slot], k_in.at[slot], y_ring(OFFSETS[slot]))

    def queries_to_pair(first, count):
        part = slots(first, count)
        qx_out[part] = dq[slots(PAIR[first], count), :].astype(BF16)
        start(f"dqx{first}", qx_out.at[part], qx_in.at[part], q_pair)

    def query_total(slot, low=0, count=H):
        total = dq[pl.ds(OWN[slot] * H + low, count), :]
        return total + qx_in[pl.ds(slot * H + low, count)].astype(F32)

    def queries_to_owner(slot):
        half = H // 2
        for at in range(2):
            part = pl.ds(at * half, half)
            total = query_total(slot, at * half, half)
            if slot == 4 - at:
                total += q_in[7, part].astype(F32)
            q_out[slot, part] = total.astype(BF16)
            if slot == 7:
                start(f"dq7{at}", q_out.at[7, part], q_in.at[7, part], z_ring(2 - 4 * at))
        if slot != 7:
            start(f"dq{slot}", q_out.at[slot], q_in.at[slot], z_ring(OFFSETS[slot]))

    arrived("c3")
    tiles(0, 4, 7)
    swap(3)
    tiles(0, 4, 6)
    arrived("s3")
    keys_to_pair(7, 1)
    keys_to_pair(5, 2)
    queries_to_pair(1, 2)
    queries_to_pair(0, 1)
    wide(3, 2)
    swap(2)
    wide(3, 1)
    swap(1)
    arrived("s2")
    keys_to_pair(3, 2)
    wide(3, 0)
    queries_to_pair(7, 1)
    queries_to_pair(5, 2)
    arrived("dkx7")
    keys_to_owner(7)
    arrived("dkx5")
    keys_to_owner(5)
    keys_to_owner(6)
    arrived("s1")
    keys_to_pair(1, 2)
    arrived("dqx0", "dqx1")
    queries_to_owner(1)
    queries_to_owner(2)
    wide(2, 0)
    queries_to_pair(3, 2)
    swap(0)
    arrived("dqx7")
    queries_to_owner(7)
    arrived("dqx5")
    queries_to_owner(5)
    queries_to_owner(6)
    arrived("s0")
    keys_to_pair(0, 1)
    arrived("dkx3", "dk70", "dk71")
    keys_to_owner(3)
    keys_to_owner(4)
    arrived("dqx3", "dq70", "dq71")
    queries_to_owner(3)
    queries_to_owner(4)
    arrived("dkx1")
    keys_to_owner(1)
    keys_to_owner(2)
    last = ("dkx0",) + tuple(f"d{kind}{slot}" for kind in "qk" for slot in range(1, 8))
    last = tuple(name for name in copies if name in last)
    for name, copy in copies.items():
        if name not in last:
            copy.wait_send()

    total = query_total(0)
    for slot in range(1, 7):
        arrived(f"dq{slot}")
        total += q_in[slot].astype(F32)
    out_ref[0] = (total * scale).astype(BF16)
    arrived("dkx0")
    for slot in range(1, 7):
        arrived(f"dk{slot}")
    for which, by in enumerate((scale, 1.0)):
        total = key_total(which, 0)
        for slot in range(1, 7):
            total += k_in[slot, which].astype(F32)
        out_ref[1 + which] = (total * by).T.astype(BF16)
    for name in last:
        copies[name].wait_send()


def part(grads, *outs):
    for index, out in enumerate(outs):
        out[...] = grads[index]


COPIES = 80


def shards(queries, keys, values, attended, out_grad, logsumexp):
    vmem = pl.BlockSpec(memory_space=pltpu.VMEM)
    block = jax.ShapeDtypeStruct((H, H), BF16)
    keys_shape = pltpu.VMEM((2, H, 8 * H), BF16)
    grads = pl.pallas_call(
        kernel,
        out_shape=jax.ShapeDtypeStruct((3, H, H), BF16),
        in_specs=[pl.BlockSpec(memory_space=pl.ANY)] * 6,
        out_specs=vmem,
        scratch_shapes=[
            pltpu.VMEM((H, H), BF16),
            pltpu.VMEM((1, H), F32),
            pltpu.SemaphoreType.DMA((6,)),
            pltpu.VMEM((LEVEL, 2 * LEVEL), BF16),
            pltpu.VMEM((LEVEL, 2 * LEVEL), BF16),
            pltpu.VMEM((4 * LEVEL, 4 * H), BF16),
            pltpu.VMEM((16, 16, H), BF16),
            pltpu.VMEM((8 * LEVEL, 4 * H), BF16),
            pltpu.VMEM((4 * LEVEL, H), F32),
            pltpu.VMEM((H, 8 * LEVEL), F32),
            pltpu.VMEM((H, 8 * LEVEL), F32),
            pltpu.VMEM((4 * LEVEL, LEVEL), BF16),
            pltpu.VMEM((4 * LEVEL, LEVEL), BF16),
            pltpu.VMEM((4, 2, H, LEVEL), BF16),
            pltpu.VMEM((4, 2, H, LEVEL), BF16),
            keys_shape,
            keys_shape,
            pltpu.VMEM((8, 2, H, H), BF16),
            pltpu.VMEM((8, 2, H, H), BF16),
            pltpu.VMEM((8 * H, H), BF16),
            pltpu.VMEM((8 * H, H), BF16),
            pltpu.VMEM((8, H, H), BF16),
            pltpu.VMEM((8, H, H), BF16),
            pltpu.SemaphoreType.DMA((COPIES,)),
            pltpu.SemaphoreType.DMA((COPIES,)),
        ],
        compiler_params=pltpu.CompilerParams(
            collective_id=0, has_side_effects=True, vmem_limit_bytes=56 * 2**20
        ),
    )(queries, keys, values, attended, out_grad, logsumexp.reshape(1, H))
    return pl.pallas_call(
        part, out_shape=(block, block, block), in_specs=[vmem], out_specs=[vmem] * 3
    )(grads)


def solution(mesh):
    rows, flat = P(("outer", "inner"), None), P(("outer", "inner"))
    return jax.shard_map(
        shards,
        mesh=mesh,
        in_specs=(rows, rows, rows, rows, rows, flat),
        out_specs=(rows, rows, rows),
        check_vma=False,
    )
```

```python
import jax
import jax.numpy as jnp
from jax import lax
from jax.experimental import pallas as pl
from jax.experimental.pallas import tpu as pltpu
from jax.sharding import PartitionSpec as P

MESH = pl.DeviceIdType.MESH
F32, BF16 = jnp.float32, jnp.bfloat16
H = 128
LEVEL = 4 * H
OFFSETS = (0, -1, 1, -2, 2, -3, 3, 4)
OWN = (0, 2, 3, 4, 5, 8, 9, 12)
PAIR = (1, 6, 7, 10, 11, 13, 14, 15)
LOG2E = 1.4426950408889634


def dot(a, b, over_a, over_b):
    return lax.dot_general(
        a, b, (((over_a,), (over_b,)), ((), ())), preferred_element_type=F32
    )


def thirds(row):
    high = row.astype(BF16).astype(F32)
    rest = row - high
    middle = rest.astype(BF16).astype(F32)
    return high, middle, rest - middle


def kernel(
    q_ref, k_ref, v_ref, a_ref, g_ref, l_ref,
    out_ref,
    own_a, own_l, load, pw, dw,
    qg, qs, kg, dq, dk, dv, pb, db,
    c_out, c_in, kx_out, kx_in, k_out, k_in, qx_out, qx_in, q_out, q_in,
    send, recv,
):
    scale = H ** (-0.5)
    outer, inner = lax.axis_index("outer"), lax.axis_index("inner")
    x, z_lo = outer % 4, outer // 4
    y, z_hi, core = inner // 4, (inner // 2) % 2, inner % 2
    z = z_hi * 4 + z_lo

    def device(x, y, z, core):
        return ((z % 4) * 4 + x, y * 4 + (z // 4) * 2 + core)

    sibling = device(x, y, z, 1 - core)
    q_pair = device(x + 1 - 2 * (x % 2), y, z, core)
    k_pair = device(3 - x, y, z, core)

    def z_ring(offset):
        return device(x, y, (z + offset + 8) % 8, core)

    def y_ring(offset):
        return device(x, (y + offset + 8) % 8, z, core)

    barrier = pltpu.get_barrier_semaphore()
    others = [sibling, q_pair, k_pair]
    others += [z_ring(offset) for offset in OFFSETS[1:]]
    others += [y_ring(offset) for offset in OFFSETS[1:7]]
    for other in others:
        pl.semaphore_signal(barrier, inc=1, device_id=other, device_id_type=MESH)

    copies = {}

    def start(name, src, dst, to):
        index = len(copies)
        copies[name] = pltpu.make_async_remote_copy(
            src_ref=src, dst_ref=dst, send_sem=send.at[index], recv_sem=recv.at[index],
            device_id=to, device_id_type=MESH,
        )
        copies[name].start()

    def arrived(*names):
        for name in names:
            copies[name].wait_recv()

    main = pl.ds(H, 2 * H)
    mine, low, high = pl.ds(0, H), pl.ds(H, H), pl.ds(2 * H, H)
    loads = [
        pltpu.make_async_copy(src, dst, load.at[index])
        for index, (src, dst) in enumerate(
            (
                (q_ref, qg.at[mine, low]), (g_ref, qg.at[mine, high]), (k_ref, kg.at[mine, low]),
                (v_ref, kg.at[mine, high]), (a_ref, own_a), (l_ref, own_l),
            )
        )
    ]
    for copy in loads:
        copy.start()
    for copy in loads:
        copy.wait()
    pl.semaphore_wait(barrier, len(others))

    def key_rows(block, count):
        return pl.ds((block // 4) * 2 * LEVEL + (block % 4) * H, count * H)

    def send_rows(name, src, dst, count, to):
        start(
            name, qg.at[pl.ds(src * H, count * H), main], qg.at[pl.ds(dst * H, count * H), main], to
        )

    def send_stats(name, src, dst, count, to):
        start(name + "s", qs.at[pl.ds(src, count)], qs.at[pl.ds(dst, count)], to)

    def send_keys(name, src, dst, count, to):
        start(name, kg.at[key_rows(src, count), main], kg.at[key_rows(dst, count), main], to)

    def share_keys(level):
        here, there = level * 2 * LEVEL, (level * 2 + 1) * LEVEL
        start(f"c{level}", kg.at[pl.ds(here, LEVEL), main], kg.at[pl.ds(there, LEVEL), main], sibling)

    def hand_on(slot, count):
        send_rows(f"qx{slot}", OWN[slot], PAIR[slot], count, q_pair)
        send_keys(f"kx{slot}", OWN[slot], PAIR[slot], count, k_pair)

    def send_on(slot, way):
        send_rows(f"q{slot + 2}", OWN[slot], OWN[slot + 2], 1, z_ring(way))
        send_keys(f"k{slot + 2}", OWN[slot], OWN[slot + 2], 1, y_ring(way))
        half = H // 2
        low = 0 if way > 0 else half
        there = pl.ds(OWN[7] * H + low, half)
        start(f"q7{way}", qg.at[pl.ds(OWN[slot] * H + low, half), main], qg.at[there, main], z_ring(2 * way))
        here, there = key_rows(OWN[slot], 1).start + low, key_rows(OWN[7], 1).start + low
        start(f"k7{way}", kg.at[pl.ds(here, half), main], kg.at[pl.ds(there, half), main], y_ring(2 * way))

    def hand_stats(slot, count):
        arrived(*(f"q{slot + index}s" for index in range(count)))
        send_stats(f"qx{slot}", OWN[slot], PAIR[slot], count, q_pair)

    def came(*slots):
        for slot in slots:
            arrived(f"q{slot}", f"k{slot}")

    def handed(*slots):
        for slot in slots:
            arrived(f"qx{slot}", f"kx{slot}")

    def to_ring(slot):
        send_rows(f"q{slot}", 0, OWN[slot], 1, z_ring(-OFFSETS[slot]))
        send_keys(f"k{slot}", 0, OWN[slot], 1, y_ring(-OFFSETS[slot]))

    to_ring(1)
    to_ring(2)
    send_rows("qx0", 0, PAIR[0], 1, q_pair)
    send_keys("kx0", 0, PAIR[0], 1, k_pair)
    to_ring(3)
    to_ring(4)

    product = qg[mine, high].astype(F32) * own_a[...].astype(F32)
    delta = jnp.sum(product.T, axis=0, keepdims=True)
    line = lax.broadcasted_iota(jnp.int32, (16, H), 0)
    stats = jnp.zeros((16, H), F32)
    for at, row in enumerate((*thirds(own_l[...] * (H**0.5)), *thirds(delta))):
        stats = jnp.where(line == at, row, stats)
    qs[0] = stats.astype(BF16)
    for slot in range(1, 8):
        send_stats(f"q{slot}", 0, OWN[slot], 1, z_ring(-OFFSETS[slot]))
    send_stats("qx0", 0, PAIR[0], 1, q_pair)

    lane = lax.broadcasted_iota(jnp.int32, (LEVEL, H), 1)
    minus = jnp.where(lane < 3, -1.0, 0.0).astype(BF16)

    def clear(column, _):
        rows = pl.ds(pl.multiple_of(column * LEVEL, LEVEL), LEVEL)
        kg[rows, 0:H] = minus
        kg[rows, 3 * H : 4 * H] = minus
        dk[:, rows] = jnp.zeros((H, LEVEL), F32)
        dv[:, rows] = jnp.zeros((H, LEVEL), F32)
        some = pl.ds(pl.multiple_of(column * 2 * H, 2 * H), 2 * H)
        dq[some, :] = jnp.zeros((2 * H, H), F32)

    lax.fori_loop(0, 8, clear, None)

    spread_at = lax.broadcasted_iota(jnp.int32, (16, H), 1)
    spread_l = jnp.where((line == spread_at) & (line < 3), 1.0, 0.0).astype(BF16)
    spread_d = jnp.where((line == spread_at + 3) & (line < 6), 1.0, 0.0).astype(BF16)

    def prepare(level):
        for block in range(4 * level, 4 * level + 4):
            rows = pl.ds(block * H, H)
            these = qs[block]
            qg[rows, 0:H] = dot(these, spread_l, 0, 0).astype(BF16)
            qg[rows, 3 * H : 4 * H] = dot(these, spread_d, 0, 0).astype(BF16)

    def grads_of(rows, keys, p, d):
        probs = jnp.exp2(dot(qg[rows, 0 : 2 * H], kg[keys, 0 : 2 * H], 1, 1) * (scale * LOG2E))
        shifted = dot(qg[rows, 2 * H : 4 * H], kg[keys, 2 * H : 4 * H], 1, 1)
        d[...] = (probs * shifted).astype(BF16)
        p[...] = probs.astype(BF16)
        dv[:, keys] += dot(qg[rows, 2 * H : 3 * H], p[...], 0, 0)
        dk[:, keys] += dot(qg[rows, H : 2 * H], d[...], 0, 0)
        dq[rows, :] += dot(d[...], kg[keys, H : 2 * H], 1, 0)

    def tiles(first, count, column):
        size = pl.ds(0, count * LEVEL)
        rows, keys = pl.ds(first * LEVEL, count * LEVEL), pl.ds(column * LEVEL, LEVEL)
        grads_of(rows, keys, pb.at[size], db.at[size])

    def wide(first, level):
        grads_of(pl.ds(first * LEVEL, LEVEL), pl.ds(level * 2 * LEVEL, 2 * LEVEL), pw, dw)

    came(1, 2)
    hand_on(1, 2)
    hand_stats(1, 2)
    handed(0)
    share_keys(0)
    arrived("qx0s")
    prepare(0)
    tiles(0, 1, 0)
    came(3, 4)
    send_on(3, 1)
    send_on(4, -1)
    hand_on(3, 2)
    hand_stats(3, 2)
    arrived("c0")
    tiles(0, 1, 1)
    handed(1)
    share_keys(1)
    arrived("qx1s")
    prepare(1)
    hand_stats(5, 2)
    hand_stats(7, 1)
    wide(1, 0)
    came(5, 6)
    hand_on(5, 2)
    arrived("q71", "q7-1", "k71", "k7-1")
    hand_on(7, 1)
    tiles(0, 2, 2)
    arrived("c1")
    tiles(0, 2, 3)
    handed(3)
    share_keys(2)
    arrived("qx3s")
    prepare(2)
    tiles(0, 3, 4)
    arrived("c2")
    tiles(0, 3, 5)
    handed(5, 7)
    share_keys(3)
    arrived("qx5s", "qx7s")
    prepare(3)
    wide(2, 1)

    def swap(level):
        theirs = pl.ds((2 * level + 1) * LEVEL, LEVEL)
        c_out[level, 0] = dk[:, theirs].astype(BF16)
        c_out[level, 1] = dv[:, theirs].astype(BF16)
        start(f"s{level}", c_out.at[level], c_in.at[level], sibling)

    def key_sum(which, block, count):
        grads = (dk, dv)[which]
        level, part = block // 4, pl.ds((block % 4) * H, count * H)
        here = pl.ds(level * 2 * LEVEL + (block % 4) * H, count * H)
        return grads[:, here] + c_in[level, which, :, part].astype(F32)

    def slots(first, count):
        return pl.ds(first * H, count * H)

    def keys_to_pair(first, count):
        part = slots(first, count)
        for which in range(2):
            kx_out[which, :, part] = key_sum(which, PAIR[first], count).astype(BF16)
        start(f"dkx{first}", kx_out.at[:, :, part], kx_in.at[:, :, part], k_pair)

    def key_total(which, slot):
        total = key_sum(which, OWN[slot], 1) + kx_in[which, :, slots(slot, 1)].astype(F32)
        if slot in (3, 4) and which == 4 - slot:
            total += k_in[7, which].astype(F32)
        return total

    def keys_to_owner(slot):
        for which in range(2):
            k_out[slot, which] = key_total(which, slot).astype(BF16)
        if slot == 7:
            for which, to in enumerate((2, -2)):
                start(f"dk7{which}", k_out.at[7, which], k_in.at[7, which], y_ring(to))
        else:
            start(f"dk{slot}", k_out.at[slot], k_in.at[slot], y_ring(OFFSETS[slot]))

    def queries_to_pair(first, count):
        part = slots(first, count)
        qx_out[part] = dq[slots(PAIR[first], count), :].astype(BF16)
        start(f"dqx{first}", qx_out.at[part], qx_in.at[part], q_pair)

    def query_total(slot, low=0, count=H):
        total = dq[pl.ds(OWN[slot] * H + low, count), :]
        return total + qx_in[pl.ds(slot * H + low, count)].astype(F32)

    def queries_to_owner(slot):
        half = H // 2
        for at in range(2):
            part = pl.ds(at * half, half)
            total = query_total(slot, at * half, half)
            if slot == 4 - at:
                total += q_in[7, part].astype(F32)
            q_out[slot, part] = total.astype(BF16)
            if slot == 7:
                start(f"dq7{at}", q_out.at[7, part], q_in.at[7, part], z_ring(2 - 4 * at))
        if slot != 7:
            start(f"dq{slot}", q_out.at[slot], q_in.at[slot], z_ring(OFFSETS[slot]))

    arrived("c3")
    tiles(0, 4, 7)
    swap(3)
    tiles(0, 4, 6)
    arrived("s3")
    keys_to_pair(7, 1)
    keys_to_pair(5, 2)
    queries_to_pair(1, 2)
    queries_to_pair(0, 1)
    wide(3, 2)
    swap(2)
    wide(3, 1)
    swap(1)
    arrived("s2")
    keys_to_pair(3, 2)
    wide(3, 0)
    queries_to_pair(7, 1)
    queries_to_pair(5, 2)
    arrived("dkx7")
    keys_to_owner(7)
    arrived("dkx5")
    keys_to_owner(5)
    keys_to_owner(6)
    arrived("s1")
    keys_to_pair(1, 2)
    arrived("dqx0", "dqx1")
    queries_to_owner(1)
    queries_to_owner(2)
    wide(2, 0)
    queries_to_pair(3, 2)
    swap(0)
    arrived("dqx7")
    queries_to_owner(7)
    arrived("dqx5")
    queries_to_owner(5)
    queries_to_owner(6)
    arrived("s0")
    keys_to_pair(0, 1)
    arrived("dkx3", "dk70", "dk71")
    keys_to_owner(3)
    keys_to_owner(4)
    arrived("dqx3", "dq70", "dq71")
    queries_to_owner(3)
    queries_to_owner(4)
    arrived("dkx1")
    keys_to_owner(1)
    keys_to_owner(2)
    last = ("dkx0",) + tuple(f"d{kind}{slot}" for kind in "qk" for slot in range(1, 8))
    last = tuple(name for name in copies if name in last)
    for name, copy in copies.items():
        if name not in last:
            copy.wait_send()

    total = query_total(0)
    for slot in range(1, 7):
        arrived(f"dq{slot}")
        total += q_in[slot].astype(F32)
    out_ref[0] = (total * scale).astype(BF16)
    arrived("dkx0")
    for slot in range(1, 7):
        arrived(f"dk{slot}")
    for which, by in enumerate((scale, 1.0)):
        total = key_total(which, 0)
        for slot in range(1, 7):
            total += k_in[slot, which].astype(F32)
        out_ref[1 + which] = (total * by).T.astype(BF16)
    for name in last:
        copies[name].wait_send()


def part(grads, *refs):
    *outs, done = refs
    copies = [
        pltpu.make_async_copy(grads.at[index], out, done.at[index])
        for index, out in enumerate(outs)
    ]
    for copy in copies:
        copy.start()
    for copy in copies:
        copy.wait()


COPIES = 80


def shards(queries, keys, values, attended, out_grad, logsumexp):
    vmem = pl.BlockSpec(memory_space=pltpu.VMEM)
    block = jax.ShapeDtypeStruct((H, H), BF16)
    keys_shape = pltpu.VMEM((2, H, 8 * H), BF16)
    grads = pl.pallas_call(
        kernel,
        out_shape=jax.ShapeDtypeStruct((3, H, H), BF16),
        in_specs=[pl.BlockSpec(memory_space=pl.ANY)] * 6,
        out_specs=vmem,
        scratch_shapes=[
            pltpu.VMEM((H, H), BF16),
            pltpu.VMEM((1, H), F32),
            pltpu.SemaphoreType.DMA((6,)),
            pltpu.VMEM((LEVEL, 2 * LEVEL), BF16),
            pltpu.VMEM((LEVEL, 2 * LEVEL), BF16),
            pltpu.VMEM((4 * LEVEL, 4 * H), BF16),
            pltpu.VMEM((16, 16, H), BF16),
            pltpu.VMEM((8 * LEVEL, 4 * H), BF16),
            pltpu.VMEM((4 * LEVEL, H), F32),
            pltpu.VMEM((H, 8 * LEVEL), F32),
            pltpu.VMEM((H, 8 * LEVEL), F32),
            pltpu.VMEM((4 * LEVEL, LEVEL), BF16),
            pltpu.VMEM((4 * LEVEL, LEVEL), BF16),
            pltpu.VMEM((4, 2, H, LEVEL), BF16),
            pltpu.VMEM((4, 2, H, LEVEL), BF16),
            keys_shape,
            keys_shape,
            pltpu.VMEM((8, 2, H, H), BF16),
            pltpu.VMEM((8, 2, H, H), BF16),
            pltpu.VMEM((8 * H, H), BF16),
            pltpu.VMEM((8 * H, H), BF16),
            pltpu.VMEM((8, H, H), BF16),
            pltpu.VMEM((8, H, H), BF16),
            pltpu.SemaphoreType.DMA((COPIES,)),
            pltpu.SemaphoreType.DMA((COPIES,)),
        ],
        compiler_params=pltpu.CompilerParams(
            collective_id=0, has_side_effects=True, vmem_limit_bytes=56 * 2**20
        ),
    )(queries, keys, values, attended, out_grad, logsumexp.reshape(1, H))
    return pl.pallas_call(
        part,
        out_shape=(block, block, block),
        in_specs=[pl.BlockSpec(memory_space=pl.ANY)],
        out_specs=[pl.BlockSpec(memory_space=pl.ANY)] * 3,
        scratch_shapes=[pltpu.SemaphoreType.DMA((3,))],
    )(grads)


def solution(mesh):
    rows, flat = P(("outer", "inner"), None), P(("outer", "inner"))
    return jax.shard_map(
        shards,
        mesh=mesh,
        in_specs=(rows, rows, rows, rows, rows, flat),
        out_specs=(rows, rows, rows),
        check_vma=False,
    )
```
